32 devices in a mesh: bx: 16 (over z, y, x), by: 2 (over core).
Axes of the slice: x: 2, y: 2, z: 4, core: 2. Of those that a mesh axis runs over, the one named last changes fastest.
Arguments:
- density: float32 [4, 128, 256], P(None, 'bx', 'by'), may hold values from 0.7 to 1.4
- velocity: float32 [3, 4, 128, 256], P(None, None, 'bx', 'by'), may hold values from -4 to 4
- pressure: float32 [4, 128, 256], P(None, 'bx', 'by'), may hold values from 0.7 to 1.4
- field: float32 [3, 4, 128, 256], P(None, None, 'bx', 'by'), may hold values from -4 to 4
Outputs:
- new_density: float32 [4, 128, 256], P(None, 'bx', 'by')
- new_momentum: float32 [3, 4, 128, 256], P(None, None, 'bx', 'by')
- new_energy: float32 [4, 128, 256], P(None, 'bx', 'by')
- new_field: float32 [3, 4, 128, 256], P(None, None, 'bx', 'by')
- time_step: float32 [], replicated
The draws below stay inside these ranges and needn't reach their ends.
All inputs are finite; a program needn't handle non-finite values.
Results may differ from the reference program's by a relative error of at most 0.0003.
Values sent between devices are 32-bit elements; how exact they have to be, the bound alone decides.
A program may use at most 64 MiB of HBM per device.

```python
import math
import jax
import jax.numpy as jnp
from jax import lax

CX = 8
CZ = 4
NX = 128
NY = 256
N_BX = 16


def shard_levels(stream_key, shape, shards, least, high):
    def one(position, parts):
        draws = jax.random.uniform(jax.random.fold_in(jax.random.fold_in(stream_key, 6), position), (parts,), jnp.float32, least / len(shards), high / len(shards))
        return jnp.repeat(jnp.exp(draws), shape[position] // parts).reshape((-1,) + (1,) * (len(shape) - position - 1))

    loudness = one(*shards[0])
    for cut in shards[1:]:
        loudness = loudness * one(*cut)
    return loudness


def centred(stream_key, shape, deviation, reach, pieces=(), kind=jnp.bfloat16):
    factor_of = shard_levels(stream_key, shape, pieces, -0.22, 0.18) if pieces else 1.0
    values = jax.random.normal(stream_key, shape, jnp.float32) * deviation * factor_of
    return jnp.minimum(jnp.maximum(values, -reach), reach).astype(kind)


def setup_inputs(seed: int = 0) -> dict:
    key_list = jax.random.split(jax.random.key(seed), 5)
    return {
        "density": jnp.clip(jnp.exp(math.log(1.4) - 0.6931472 * jax.random.uniform(key_list[0], (CZ, NX, NY), jnp.float32) ** shard_levels(key_list[0], (CZ, NX, NY), ((1, 16), (2, 2)), -0.2, 0.2)), 0.7, 1.4),
        "velocity": centred(key_list[1], (3, CZ, NX, NY), 0.3, 4.0, ((2, 16), (3, 2)), jnp.float32),
        "pressure": jnp.clip(jnp.exp(math.log(1.4) - 0.6931472 * jax.random.uniform(key_list[2], (CZ, NX, NY), jnp.float32) ** shard_levels(key_list[2], (CZ, NX, NY), ((1, 16), (2, 2)), -0.2, 0.2)), 0.7, 1.4),
        "field": centred(key_list[3], (3, CZ, NX, NY), 0.3, 4.0, ((2, 16), (3, 2)), jnp.float32),
    }


GAMMA = 5.0 / 3.0
CFL = 0.3
AXES = (1, 2, 0)
deep_rim = 7

def moved(array, by, comp):
    return jnp.roll(array, by, AXES[comp])

def fast_speed(rho, pres, normal, trans_one, trans_two):
    sound = GAMMA * pres / rho
    along = normal * normal / rho
    across = (trans_one * trans_one + trans_two * trans_two) / rho
    inner = (sound - along) ** 2 + across * (across + 2.0 * sound + 2.0 * along)
    return jnp.sqrt(0.5 * (sound + along + across + jnp.sqrt(inner)))

def centered(face):
    return [0.5 * (face[c] + moved(face[c], -1, c)) for c in range(3)]

def unpack(stack):
    return (stack[0], [stack[1], stack[2], stack[3]], stack[4], [stack[5], stack[6], stack[7]])

def speeds(stack):
    rho, vel, pres, face = unpack(stack)
    cell = centered(face)
    best = None
    for c in range(3):
        value = jnp.abs(vel[c]) + fast_speed(rho, pres, cell[c], cell[(c + 1) % 3], cell[(c + 2) % 3])
        best = value if best is None else jnp.maximum(best, value)
    return best

def conserved(rho, vel, pres, cell):
    bsq = cell[0] * cell[0] + cell[1] * cell[1] + cell[2] * cell[2]
    vsq = vel[0] * vel[0] + vel[1] * vel[1] + vel[2] * vel[2]
    energy = pres / (GAMMA - 1.0) + 0.5 * rho * vsq + 0.5 * bsq
    return [rho, rho * vel[0], rho * vel[1], rho * vel[2], energy]

def side_terms(prim, normal, comp):
    rho, vel, pres = (prim[0], prim[1:4], prim[4])
    mag = list(prim[5:8])
    mag[comp] = normal
    one, two = ((comp + 1) % 3, (comp + 2) % 3)
    bsq = mag[0] * mag[0] + mag[1] * mag[1] + mag[2] * mag[2]
    total = pres + 0.5 * bsq
    cons = conserved(rho, vel, pres, mag)
    vnorm = vel[comp]
    vdotb = vel[0] * mag[0] + vel[1] * mag[1] + vel[2] * mag[2]
    flux = [rho * vnorm]
    for k in range(3):
        term = rho * vel[k] * vnorm - mag[k] * normal
        flux.append(term + total if k == comp else term)
    flux.append((cons[4] + total) * vnorm - normal * vdotb)
    flux.append(mag[one] * vnorm - normal * vel[one])
    flux.append(mag[two] * vnorm - normal * vel[two])
    cons = cons + [mag[one], mag[two]]
    return (cons, flux, vnorm, fast_speed(rho, pres, normal, mag[one], mag[two]))

def hlle(left, right, normal, comp):
    cons_left, flux_left, vel_left, fast_left = side_terms(left, normal, comp)
    cons_right, flux_right, vel_right, fast_right = side_terms(right, normal, comp)
    lower = jnp.minimum(jnp.minimum(vel_left - fast_left, vel_right - fast_right), 0.0)
    upper = jnp.maximum(jnp.maximum(vel_left + fast_left, vel_right + fast_right), 0.0)
    spread = upper - lower
    return [(upper * flux_left[v] - lower * flux_right[v] + lower * upper * (cons_right[v] - cons_left[v])) / spread for v in range(7)]

def minmod(first, second):
    return jnp.where(first * second > 0.0, jnp.sign(first) * jnp.minimum(jnp.abs(first), jnp.abs(second)), 0.0)

def fluxes(stack, slopes):
    rho, vel, pres, face = unpack(stack)
    cell = centered(face)
    prim = [rho, vel[0], vel[1], vel[2], pres, cell[0], cell[1], cell[2]]
    result = []
    for c in range(3):
        if slopes:
            grads = [minmod(q - moved(q, 1, c), moved(q, -1, c) - q) for q in prim]
            left = [moved(q + 0.5 * g, 1, c) for q, g in zip(prim, grads)]
            right = [q - 0.5 * g for q, g in zip(prim, grads)]
        else:
            left = [moved(q, 1, c) for q in prim]
            right = prim
        result.append(hlle(left, right, face[c], c))
    return result

def changes(flux):
    div = []
    for v in range(5):
        total = None
        for c in range(3):
            term = moved(flux[c][v], -1, c) - flux[c][v]
            total = term if total is None else total + term
        div.append(total)
    fx, fy, fz = flux
    ez = 0.25 * (-fx[5] - moved(fx[5], 1, 1) + fy[6] + moved(fy[6], 1, 0))
    ex = 0.25 * (-fy[5] - moved(fy[5], 1, 2) + fz[6] + moved(fz[6], 1, 1))
    ey = 0.25 * (-fz[5] - moved(fz[5], 1, 0) + fx[6] + moved(fx[6], 1, 2))
    curl = [moved(ez, -1, 1) - ez - (moved(ey, -1, 2) - ey), moved(ex, -1, 2) - ex - (moved(ez, -1, 0) - ez), moved(ey, -1, 0) - ey - (moved(ex, -1, 1) - ex)]
    return (div, curl)

def base(stack):
    rho, vel, pres, face = unpack(stack)
    start = conserved(rho, vel, pres, centered(face))
    return jnp.stack(start + face)

def half_state(stack, step):
    rho, vel, pres, face = unpack(stack)
    start = conserved(rho, vel, pres, centered(face))
    div, curl = changes(fluxes(stack, False))
    cons = [start[v] - 0.5 * step * div[v] for v in range(5)]
    newface = [face[c] - 0.5 * step * curl[c] for c in range(3)]
    cell = centered(newface)
    hrho = cons[0]
    hvel = [cons[k + 1] / hrho for k in range(3)]
    msq = cons[1] * cons[1] + cons[2] * cons[2] + cons[3] * cons[3]
    bsq = cell[0] * cell[0] + cell[1] * cell[1] + cell[2] * cell[2]
    hpres = (GAMMA - 1.0) * (cons[4] - 0.5 * msq / hrho - 0.5 * bsq)
    return jnp.stack([hrho] + hvel + [hpres] + newface)

def correction(half):
    div, curl = changes(fluxes(half, True))
    return jnp.stack(div + curl)

def reference(density, velocity, pressure, field):
    stack = jnp.concatenate([density[None], velocity, pressure[None], field], axis=0)
    padded = jnp.concatenate([stack[:, :, NX - deep_rim:], stack, stack[:, :, :deep_rim]], axis=2)
    starts = jnp.arange(N_BX, dtype=jnp.int32) * CX

    def block(start):
        return lax.dynamic_slice_in_dim(padded, start.astype(jnp.int32), CX + 2 * deep_rim, 2)

    def block_top(start):
        return jnp.max(speeds(block(start))[:, deep_rim:-deep_rim, :])
    top = jnp.max(lax.map(block_top, starts))
    step = CFL / top

    def block_step(start):
        wide = block(start)
        half = half_state(wide, step)
        final = base(wide) - step * correction(half)
        return final[:, :, deep_rim:-deep_rim, :]
    outs = lax.map(block_step, starts)
    whole = jnp.transpose(outs, (1, 2, 0, 3, 4)).reshape(8, CZ, NX, NY)
    return (whole[0], whole[1:4], whole[4], whole[5:8], step)
```

```python
import functools

import jax
import jax.numpy as jnp
from jax import lax
from jax.experimental import pallas as pl
from jax.experimental.pallas import tpu as pltpu
from jax.sharding import PartitionSpec as P

GAMMA = 5.0 / 3.0
CFL = 0.3
TINY = 1e-30
CZ, CX, CY = 4, 8, 128
EDGE = 4
CHUNKS = 5
HALOS = ((1, 0), (-1, 0), (0, 1), (0, -1), (1, 1), (1, -1), (-1, 1), (-1, -1))


def max_stages(nbx, nby):
    stages = [[(0, o) for o in range(1, nby)]]
    window = 1
    while window < nbx:
        stages.append([(m * window, 0) for m in (1, 2, 3) if m * window < nbx])
        window *= 4
    return [s for s in stages if s]


def roll(a, by, axis):
    by = by % a.shape[axis]
    return a if by == 0 else pltpu.roll(a, by, axis)


def lanes():
    return lax.broadcasted_iota(jnp.int32, (1, CY), 1)


def shifted(ref, v, k, by, c):
    if c == 0:
        return roll(ref[v, k], by, 0)
    if c == 2:
        return ref[v, (k - by) % CZ] if k < EDGE else roll(ref[v, k], 32 * by, 1)
    body = roll(ref[v, k], by, 1)
    if k == EDGE:
        return body
    if by == 1:
        return jnp.where(lanes() == 0, roll(ref[v, EDGE], -(32 * k + 7), 1), body)
    return jnp.where(lanes() == CY - 1, roll(ref[v, EDGE], CY - 1 - (32 * k + 24), 1), body)


def root(y):
    return y * lax.rsqrt(jnp.maximum(y, TINY))


def fast(rho, pres, n, t):
    a = GAMMA * pres
    s = a + n
    d = a - n
    x = 0.5 * (s + t + root(d * d + t * (t + 2.0 * s)))
    return x * lax.rsqrt(jnp.maximum(x * rho, TINY))


def part(side, bn, n, fastness, alpha_term, w):
    rho, vn, v1, v2, p, b1, b2, t = side
    half_bsq = 0.5 * (t + n)
    energy = 1.5 * p + (0.5 * rho) * (vn * vn + v1 * v1 + v2 * v2) + half_bsq
    wp = w * (p + half_bsq)
    beta = w * bn
    alpha = w * vn + alpha_term
    m = alpha * rho
    vb = vn * bn + v1 * b1 + v2 * b2
    return [
        m,
        m * vn - beta * bn + wp,
        m * v1 - beta * b1,
        m * v2 - beta * b2,
        alpha * energy + wp * vn - beta * vb,
        alpha * b1 - beta * v1,
        alpha * b2 - beta * v2,
    ]


def hlle(left, right, bn):
    n = bn * bn
    left = left + [left[5] * left[5] + left[6] * left[6]]
    right = right + [right[5] * right[5] + right[6] * right[6]]
    cl = fast(left[0], left[4], n, left[7])
    cr = fast(right[0], right[4], n, right[7])
    sl = jnp.minimum(jnp.minimum(left[1] - cl, right[1] - cr), 0.0)
    sr = jnp.maximum(jnp.maximum(left[1] + cl, right[1] + cr), 0.0)
    inv = 1.0 / (sr - sl)
    wl = sr * inv
    wr = -sl * inv
    wd = sl * wl
    fl = part(left, bn, n, cl, -wd, wl)
    fr = part(right, bn, n, cr, wd, wr)
    return [a + b for a, b in zip(fl, fr)]


def put_flux(flux, c, k, values):
    one, two = (c + 1) % 3, (c + 2) % 3
    for slot, value in zip((0, 1 + c, 1 + one, 1 + two, 4, 5, 6), values):
        flux[7 * c + slot, k] = value


def curl_parts(edge, c, k):
    one, two = (c + 1) % 3, (c + 2) % 3
    return (shifted(edge, two, k, -1, one) - edge[two, k]) - (
        shifted(edge, one, k, -1, two) - edge[one, k]
    )


def edges(flux, edge, ks):
    for k in ks:
        for e in range(3):
            a, b = (e + 1) % 3, (e + 2) % 3
            fa, fb = 7 * a + 5, 7 * b + 6
            edge[e, k] = 0.25 * (
                (flux[fb, k] + shifted(flux, fb, k, 1, a))
                - (flux[fa, k] + shifted(flux, fa, k, 1, b))
            )


def div_part(flux, v, k):
    total = None
    for c in range(3):
        term = shifted(flux, 7 * c + v, k, -1, c) - flux[7 * c + v, k]
        total = term if total is None else total + term
    return total


def strips(tiles):
    lane = lanes()
    merged = roll(tiles[0], 8, 1)
    for z in range(1, CZ):
        merged = jnp.where(lane >= 32 * z, roll(tiles[z], 8 + 32 * z, 1), merged)
    return jnp.where(lane % 32 < 16, merged, roll(merged, 16, 1))


def kernel(
    nbx, nby, stages,
    rho_in, vel_in, pres_in, face_in,
    rho_out, mom_out, ener_out, face_out, step_out,
    own, own_strip, halo, y_strip, d_strip, top_send, top_recv,
    state, cell, flux, edge, change, half, hcell, lefts, rights, result,
    in_sem, out_sem, send_sem, recv_sem, tsend_sem, trecv_sem,
):
    mx, my = lax.axis_index("bx"), lax.axis_index("by")

    def at(dx, dy):
        return (lax.rem(mx + dx % nbx, nbx), lax.rem(my + dy % nby, nby))

    loads = [
        pltpu.make_async_copy(rho_in, own.at[0], in_sem.at[0]),
        pltpu.make_async_copy(vel_in, own.at[pl.ds(1, 3)], in_sem.at[1]),
        pltpu.make_async_copy(pres_in, own.at[4], in_sem.at[2]),
        pltpu.make_async_copy(face_in, own.at[pl.ds(5, 3)], in_sem.at[3]),
    ]
    for copy in loads:
        copy.start()

    barrier = pltpu.get_barrier_semaphore()
    greeted = sorted(
        {(dx % nbx, dy % nby) for dx, dy in HALOS}
        | {((-dx) % nbx, (-dy) % nby) for stage in stages for dx, dy in stage}
    )
    for dx, dy in greeted:
        pl.semaphore_signal(
            barrier, inc=1, device_id=at(dx, dy), device_id_type=pl.DeviceIdType.MESH
        )
    for copy in loads:
        copy.wait()
    for v in range(8):
        own_strip[v] = strips([own[v, z] for z in range(CZ)])
    pl.semaphore_wait(barrier, len(greeted))

    low, high = pl.ds(0, 4), pl.ds(4, 4)
    plan = [
        (own.at[:, :, high, :], halo.at[:, :, high, :]),
        (own.at[:, :, low, :], halo.at[:, :, low, :]),
        (own_strip, y_strip.at[0]),
        (own_strip, y_strip.at[1]),
        (own_strip.at[:, high, :], d_strip.at[0, :, high, :]),
        (own_strip.at[:, high, :], d_strip.at[1, :, high, :]),
        (own_strip.at[:, low, :], d_strip.at[0, :, low, :]),
        (own_strip.at[:, low, :], d_strip.at[1, :, low, :]),
    ]
    sends = [
        pltpu.make_async_remote_copy(
            src_ref=src, dst_ref=dst, send_sem=send_sem.at[i], recv_sem=recv_sem.at[i],
            device_id=at(*HALOS[i]), device_id_type=pl.DeviceIdType.MESH,
        )
        for i, (src, dst) in enumerate(plan)
    ]
    for copy in sends:
        copy.start()
    for copy in sends:
        copy.wait_recv()

    lane = lanes() % 32
    for v in range(8):
        for z in range(CZ):
            state[v, z, 0:8] = own[v, z]
            state[v, z, 8:16] = halo[v, z]
        state[v, EDGE, 0:8] = jnp.where(
            lane < 8, y_strip[0, v], jnp.where(lane < 24, own_strip[v], y_strip[1, v])
        )
        state[v, EDGE, 8:16] = jnp.where(
            lane < 8,
            d_strip[0, v],
            jnp.where(lane < 24, strips([halo[v, z] for z in range(CZ)]), d_strip[1, v]),
        )
    for k in range(CHUNKS):
        for c in range(3):
            cell[c, k] = 0.5 * (state[5 + c, k] + shifted(state, 5 + c, k, -1, c))

    best = None
    for z in range(CZ):
        rho, pres = state[0, z, 0:8], state[4, z, 0:8]
        sq = [cell[c, z, 0:8] * cell[c, z, 0:8] for c in range(3)]
        for c in range(3):
            value = jnp.abs(state[1 + c, z, 0:8]) + fast(
                rho, pres, sq[c], sq[(c + 1) % 3] + sq[(c + 2) % 3]
            )
            best = value if best is None else jnp.maximum(best, value)
    top = jnp.max(best, axis=0, keepdims=True)

    first_slot = [sum(len(s) for s in stages[:i]) for i in range(len(stages))]
    started = []

    def stage_start(i, value):
        top_send[i] = value
        copies = []
        for j, (dx, dy) in enumerate(stages[i]):
            slot = first_slot[i] + j
            copy = pltpu.make_async_remote_copy(
                src_ref=top_send.at[i], dst_ref=top_recv.at[slot],
                send_sem=tsend_sem.at[slot], recv_sem=trecv_sem.at[slot],
                device_id=at(dx, dy), device_id_type=pl.DeviceIdType.MESH,
            )
            copy.start()
            copies.append(copy)
        started.append(copies)

    def stage_end(i, value):
        for copy in started[i]:
            copy.wait_recv()
        for j in range(len(stages[i])):
            value = jnp.maximum(value, top_recv[first_slot[i] + j])
        return value

    stage_start(0, top)
    for c in range(3):
        one, two = (c + 1) % 3, (c + 2) % 3
        for k in range(CHUNKS):
            names = [(state, 0), (state, 1 + c), (state, 1 + one), (state, 1 + two), (state, 4),
                     (cell, one), (cell, two)]
            left = [shifted(ref, v, k, 1, c) for ref, v in names]
            right = [ref[v, k] for ref, v in names]
            put_flux(flux, c, k, hlle(left, right, state[5 + c, k]))
        if c + 1 < min(3, len(stages)):
            top = stage_end(c, top)
            stage_start(c + 1, top)
    edges(flux, edge, range(CHUNKS))
    for k in range(CHUNKS):
        for v in range(5):
            change[v, k] = div_part(flux, v, k)
        for c in range(3):
            change[5 + c, k] = curl_parts(edge, c, k)
    for i in range(min(3, len(stages)) - 1, len(stages)):
        top = stage_end(i, top)
        if i + 1 < len(stages):
            stage_start(i + 1, top)
    step = CFL / jnp.broadcast_to(jnp.max(top, axis=1, keepdims=True), (1, CY))
    step_out[0] = jnp.max(step)
    semi = 0.5 * step

    for k in range(CHUNKS):
        for c in range(3):
            half[5 + c, k] = state[5 + c, k] - semi * change[5 + c, k]
    for k in range(CHUNKS):
        rho, pres = state[0, k], state[4, k]
        vel = [state[1 + c, k] for c in range(3)]
        mag = [cell[c, k] for c in range(3)]
        energy = (
            1.5 * pres
            + (0.5 * rho) * (vel[0] * vel[0] + vel[1] * vel[1] + vel[2] * vel[2])
            + 0.5 * (mag[0] * mag[0] + mag[1] * mag[1] + mag[2] * mag[2])
        )
        if k < EDGE:
            result[0, k] = energy[0:8]
        hrho = rho - semi * change[0, k]
        inv = 1.0 / hrho
        mom = [rho * vel[c] - semi * change[1 + c, k] for c in range(3)]
        energy = energy - semi * change[4, k]
        hmag = [0.5 * (half[5 + c, k] + shifted(half, 5 + c, k, -1, c)) for c in range(3)]
        msq = mom[0] * mom[0] + mom[1] * mom[1] + mom[2] * mom[2]
        bsq = hmag[0] * hmag[0] + hmag[1] * hmag[1] + hmag[2] * hmag[2]
        half[0, k] = hrho
        for c in range(3):
            half[1 + c, k] = mom[c] * inv
            hcell[c, k] = hmag[c]
        half[4, k] = (GAMMA - 1.0) * (energy - 0.5 * (msq * inv) - 0.5 * bsq)

    for c in range(3):
        one, two = (c + 1) % 3, (c + 2) % 3
        names = [(half, 0), (half, 1 + c), (half, 1 + one), (half, 1 + two), (half, 4),
                 (hcell, one), (hcell, two)]
        for k in range(CHUNKS):
            for i, (ref, v) in enumerate(names):
                q = ref[v, k]
                a = q - shifted(ref, v, k, 1, c)
                b = shifted(ref, v, k, -1, c) - q
                g = 0.5 * (
                    jnp.maximum(jnp.minimum(a, b), 0.0) + jnp.minimum(jnp.maximum(a, b), 0.0)
                )
                lefts[7 * c + i, k] = q + g
                rights[7 * c + i, k] = q - g
        for k in range(CHUNKS):
            left = [shifted(lefts, 7 * c + i, k, 1, c) for i in range(7)]
            right = [rights[7 * c + i, k] for i in range(7)]
            put_flux(flux, c, k, hlle(left, right, half[5 + c, k]))
    edges(flux, edge, range(CHUNKS))
    for z in range(CZ):
        rho = state[0, z, 0:8]
        for v in range(5):
            start = rho if v == 0 else result[0, z] if v == 4 else rho * state[v, z, 0:8]
            value = start - step * div_part(flux, v, z)[0:8]
            if v == 0:
                rho_out[z] = value
            elif v == 4:
                ener_out[z] = value
            else:
                mom_out[v - 1, z] = value
        for c in range(3):
            face_out[c, z] = state[5 + c, z, 0:8] - step * curl_parts(edge, c, z)[0:8]

    for copy in sends:
        copy.wait_send()
    for copies in started:
        for copy in copies:
            copy.wait_send()


def on_device(nbx, nby, density, velocity, pressure, field):
    stages = max_stages(nbx, nby)
    slots = sum(len(s) for s in stages)
    f32 = jnp.float32
    wide = (CHUNKS, 2 * CX, CY)
    out = pl.pallas_call(
        functools.partial(kernel, nbx, nby, stages),
        out_shape=[
            jax.ShapeDtypeStruct((CZ, CX, CY), f32),
            jax.ShapeDtypeStruct((3, CZ, CX, CY), f32),
            jax.ShapeDtypeStruct((CZ, CX, CY), f32),
            jax.ShapeDtypeStruct((3, CZ, CX, CY), f32),
            jax.ShapeDtypeStruct((1,), f32),
        ],
        in_specs=[pl.BlockSpec(memory_space=pl.ANY)] * 4,
        out_specs=[pl.BlockSpec(memory_space=pltpu.VMEM)] * 4
        + [pl.BlockSpec(memory_space=pltpu.SMEM)],
        scratch_shapes=[
            pltpu.VMEM((8, CZ, CX, CY), f32),
            pltpu.VMEM((8, CX, CY), f32),
            pltpu.VMEM((8, CZ, CX, CY), f32),
            pltpu.VMEM((2, 8, CX, CY), f32),
            pltpu.VMEM((2, 8, CX, CY), f32),
            pltpu.VMEM((len(stages), 1, CY), f32),
            pltpu.VMEM((slots, 1, CY), f32),
            pltpu.VMEM((8,) + wide, f32),
            pltpu.VMEM((3,) + wide, f32),
            pltpu.VMEM((21,) + wide, f32),
            pltpu.VMEM((3,) + wide, f32),
            pltpu.VMEM((8,) + wide, f32),
            pltpu.VMEM((8,) + wide, f32),
            pltpu.VMEM((3,) + wide, f32),
            pltpu.VMEM((21,) + wide, f32),
            pltpu.VMEM((21,) + wide, f32),
            pltpu.VMEM((1, CZ, CX, CY), f32),
            pltpu.SemaphoreType.DMA((4,)),
            pltpu.SemaphoreType.DMA((4,)),
            pltpu.SemaphoreType.DMA((8,)),
            pltpu.SemaphoreType.DMA((8,)),
            pltpu.SemaphoreType.DMA((slots,)),
            pltpu.SemaphoreType.DMA((slots,)),
        ],
        compiler_params=pltpu.CompilerParams(
            collective_id=0, has_side_effects=True, vmem_limit_bytes=32 * 1024 * 1024
        ),
    )(density, velocity, pressure, field)
    return (out[0], out[1], out[2], out[3], out[4].reshape(()))


def solution(mesh):
    in_specs = (
        P(None, "bx", "by"),
        P(None, None, "bx", "by"),
        P(None, "bx", "by"),
        P(None, None, "bx", "by"),
    )
    out_specs = in_specs + (P(),)
    return jax.shard_map(
        functools.partial(on_device, mesh.shape["bx"], mesh.shape["by"]),
        mesh=mesh, in_specs=in_specs, out_specs=out_specs, check_vma=False,
    )
```

```python
import functools

import jax
import jax.numpy as jnp
from jax import lax
from jax.experimental import pallas as pl
from jax.experimental.pallas import tpu as pltpu
from jax.sharding import PartitionSpec as P

GAMMA = 5.0 / 3.0
CFL = 0.3
TINY = 1e-30
CZ, CX, CY = 4, 8, 128
EDGE = 4
CHUNKS = 5
HALOS = ((-1, 0), (0, -1), (1, 0), (-1, 0), (1, 1), (-1, 1), (0, 1), (1, -1), (-1, -1), (0, -1))


def max_stages(nbx, nby):
    if nbx * nby <= 32:
        return [[(x, y) for x in range(nbx) for y in range(nby) if (x, y) != (0, 0)]]
    stages = [[(0, o) for o in range(1, nby)]]
    window = 1
    while window < nbx:
        stages.append([(m * window, 0) for m in (1, 2, 3) if m * window < nbx])
        window *= 4
    return [s for s in stages if s]


def roll(a, by, axis):
    by = by % a.shape[axis]
    return a if by == 0 else pltpu.roll(a, by, axis)


def lanes():
    return lax.broadcasted_iota(jnp.int32, (1, CY), 1)


def shifted(ref, v, k, by, c):
    if c == 0:
        return roll(ref[v, k], by, 0)
    if c == 2:
        return ref[v, (k - by) % CZ] if k < EDGE else roll(ref[v, k], 32 * by, 1)
    body = roll(ref[v, k], by, 1)
    if k == EDGE:
        return body
    if by == 1:
        return jnp.where(lanes() == 0, roll(ref[v, EDGE], -(32 * k + 7), 1), body)
    return jnp.where(lanes() == CY - 1, roll(ref[v, EDGE], CY - 1 - (32 * k + 24), 1), body)


def root(y):
    return y * lax.rsqrt(jnp.maximum(y, TINY))


def fast(rho, pres, n, t):
    a = GAMMA * pres
    s = a + n
    d = a - n
    x = 0.5 * (s + t + root(d * d + t * (t + 2.0 * s)))
    return x * lax.rsqrt(jnp.maximum(x * rho, TINY))


def part(side, bn, n, fastness, alpha_term, w):
    rho, vn, v1, v2, p, b1, b2, t = side
    half_bsq = 0.5 * (t + n)
    energy = 1.5 * p + (0.5 * rho) * (vn * vn + v1 * v1 + v2 * v2) + half_bsq
    wp = w * (p + half_bsq)
    beta = w * bn
    alpha = w * vn + alpha_term
    m = alpha * rho
    vb = vn * bn + v1 * b1 + v2 * b2
    return [
        m,
        m * vn - beta * bn + wp,
        m * v1 - beta * b1,
        m * v2 - beta * b2,
        alpha * energy + wp * vn - beta * vb,
        alpha * b1 - beta * v1,
        alpha * b2 - beta * v2,
    ]


def hlle(left, right, bn):
    n = bn * bn
    left = left + [left[5] * left[5] + left[6] * left[6]]
    right = right + [right[5] * right[5] + right[6] * right[6]]
    cl = fast(left[0], left[4], n, left[7])
    cr = fast(right[0], right[4], n, right[7])
    sl = jnp.minimum(jnp.minimum(left[1] - cl, right[1] - cr), 0.0)
    sr = jnp.maximum(jnp.maximum(left[1] + cl, right[1] + cr), 0.0)
    inv = 1.0 / (sr - sl)
    wl = sr * inv
    wr = -sl * inv
    wd = sl * wl
    fl = part(left, bn, n, cl, -wd, wl)
    fr = part(right, bn, n, cr, wd, wr)
    return [a + b for a, b in zip(fl, fr)]


def put_flux(flux, c, k, values):
    one, two = (c + 1) % 3, (c + 2) % 3
    for slot, value in zip((0, 1 + c, 1 + one, 1 + two, 4, 5, 6), values):
        flux[7 * c + slot, k] = value


def curl_parts(edge, c, k):
    one, two = (c + 1) % 3, (c + 2) % 3
    return (shifted(edge, two, k, -1, one) - edge[two, k]) - (
        shifted(edge, one, k, -1, two) - edge[one, k]
    )


def edges(flux, edge, ks):
    for k in ks:
        for e in range(3):
            a, b = (e + 1) % 3, (e + 2) % 3
            fa, fb = 7 * a + 5, 7 * b + 6
            edge[e, k] = 0.25 * (
                (flux[fb, k] + shifted(flux, fb, k, 1, a))
                - (flux[fa, k] + shifted(flux, fa, k, 1, b))
            )


def div_part(flux, v, k):
    total = None
    for c in range(3):
        term = shifted(flux, 7 * c + v, k, -1, c) - flux[7 * c + v, k]
        total = term if total is None else total + term
    return total


def strips(tiles):
    lane = lanes()
    merged = roll(tiles[0], 8, 1)
    for z in range(1, CZ):
        merged = jnp.where(lane >= 32 * z, roll(tiles[z], 8 + 32 * z, 1), merged)
    return jnp.where(lane % 32 < 16, merged, roll(merged, 16, 1))


def kernel(
    nbx, nby, stages,
    rho_in, vel_in, pres_in, face_in,
    rho_out, mom_out, ener_out, face_out, step_out,
    own, own_strip, x_edge, y_edge, halo, y_strip, d_strip, top_send, top_recv,
    state, cell, flux, edge, change, half, hcell, lefts, rights, result,
    in_sem, out_sem, send_sem, recv_sem, tsend_sem, trecv_sem,
):
    mx, my = lax.axis_index("bx"), lax.axis_index("by")

    def at(dx, dy):
        return (lax.rem(mx + dx % nbx, nbx), lax.rem(my + dy % nby, nby))

    loads = [
        pltpu.make_async_copy(rho_in, own.at[0], in_sem.at[0]),
        pltpu.make_async_copy(vel_in, own.at[pl.ds(1, 3)], in_sem.at[1]),
        pltpu.make_async_copy(pres_in, own.at[4], in_sem.at[2]),
        pltpu.make_async_copy(face_in, own.at[pl.ds(5, 3)], in_sem.at[3]),
    ]
    for copy in loads:
        copy.start()

    barrier = pltpu.get_barrier_semaphore()
    greeted = sorted(
        {(dx % nbx, dy % nby) for dx, dy in HALOS}
        | {((-dx) % nbx, (-dy) % nby) for stage in stages for dx, dy in stage}
    )
    for dx, dy in greeted:
        pl.semaphore_signal(
            barrier, inc=1, device_id=at(dx, dy), device_id_type=pl.DeviceIdType.MESH
        )
    for copy in loads:
        copy.wait()
    for v in range(8):
        own_strip[v] = strips([own[v, z] for z in range(CZ)])
    pl.semaphore_wait(barrier, len(greeted))

    low, high = pl.ds(0, 4), pl.ds(4, 4)
    other = 0 if nby == 2 else 1
    plan = [
        (own.at[5, :, pl.ds(0, 1), :], x_edge.at[:, pl.ds(0, 1), :]),
        (own_strip.at[6], y_edge),
        (own.at[:, :, high, :], halo.at[:, :, high, :]),
        (own.at[:, :, low, :], halo.at[:, :, low, :]),
        (own_strip.at[:, high, :], d_strip.at[0, :, high, :]),
        (own_strip.at[:, low, :], d_strip.at[0, :, low, :]),
        (own_strip, y_strip.at[0]),
        (own_strip.at[:, high, :], d_strip.at[other, :, high, :]),
        (own_strip.at[:, low, :], d_strip.at[other, :, low, :]),
        (own_strip, y_strip.at[other]),
    ]
    if nby == 2:
        plan = plan[:7]
    sends = [
        pltpu.make_async_remote_copy(
            src_ref=src, dst_ref=dst, send_sem=send_sem.at[i], recv_sem=recv_sem.at[i],
            device_id=at(*HALOS[i]), device_id_type=pl.DeviceIdType.MESH,
        )
        for i, (src, dst) in enumerate(plan)
    ]
    for copy in sends:
        copy.start()
    for copy in sends[:2]:
        copy.wait_recv()

    best = None
    last_row = lax.broadcasted_iota(jnp.int32, (CX, 1), 0) == CX - 1
    last_lane = lanes() == CY - 1
    for z in range(CZ):
        rho, pres = own[0, z], own[4, z]
        face = [own[5 + c, z] for c in range(3)]
        after = [
            jnp.where(last_row, x_edge[z, 0:1], roll(face[0], -1, 0)),
            jnp.where(last_lane, roll(y_edge[...], CY - 1 - (32 * z + 24), 1), roll(face[1], -1, 1)),
            own[7, (z + 1) % CZ],
        ]
        mag = [0.5 * (face[c] + after[c]) for c in range(3)]
        sq = [m * m for m in mag]
        for c in range(3):
            value = jnp.abs(own[1 + c, z]) + fast(rho, pres, sq[c], sq[(c + 1) % 3] + sq[(c + 2) % 3])
            best = value if best is None else jnp.maximum(best, value)
    top = jnp.max(best, axis=0, keepdims=True)

    first_slot = [sum(len(s) for s in stages[:i]) for i in range(len(stages))]
    started = []

    def stage_start(i, value):
        top_send[i] = value
        copies = []
        for j, (dx, dy) in enumerate(stages[i]):
            slot = first_slot[i] + j
            copy = pltpu.make_async_remote_copy(
                src_ref=top_send.at[i], dst_ref=top_recv.at[slot],
                send_sem=tsend_sem.at[slot], recv_sem=trecv_sem.at[slot],
                device_id=at(dx, dy), device_id_type=pl.DeviceIdType.MESH,
            )
            copy.start()
            copies.append(copy)
        started.append(copies)

    def stage_end(i, value):
        for copy in started[i]:
            copy.wait_recv()
        for j in range(len(stages[i])):
            value = jnp.maximum(value, top_recv[first_slot[i] + j])
        return value

    stage_start(0, top)
    for copy in sends[2:]:
        copy.wait_recv()

    lane = lanes() % 32
    for v in range(8):
        for z in range(CZ):
            state[v, z, 0:8] = own[v, z]
            state[v, z, 8:16] = halo[v, z]
        state[v, EDGE, 0:8] = jnp.where(
            lane < 8, y_strip[0, v], jnp.where(lane < 24, own_strip[v], y_strip[other, v])
        )
        state[v, EDGE, 8:16] = jnp.where(
            lane < 8,
            d_strip[0, v],
            jnp.where(lane < 24, strips([halo[v, z] for z in range(CZ)]), d_strip[other, v]),
        )
    for k in range(CHUNKS):
        for c in range(3):
            cell[c, k] = 0.5 * (state[5 + c, k] + shifted(state, 5 + c, k, -1, c))

    for c in range(3):
        one, two = (c + 1) % 3, (c + 2) % 3
        for k in range(CHUNKS):
            names = [(state, 0), (state, 1 + c), (state, 1 + one), (state, 1 + two), (state, 4),
                     (cell, one), (cell, two)]
            left = [shifted(ref, v, k, 1, c) for ref, v in names]
            right = [ref[v, k] for ref, v in names]
            put_flux(flux, c, k, hlle(left, right, state[5 + c, k]))
        if c + 1 < min(3, len(stages)):
            top = stage_end(c, top)
            stage_start(c + 1, top)
    edges(flux, edge, range(CHUNKS))
    for k in range(CHUNKS):
        for v in range(5):
            change[v, k] = div_part(flux, v, k)
        for c in range(3):
            change[5 + c, k] = curl_parts(edge, c, k)
    for i in range(min(3, len(stages)) - 1, len(stages)):
        top = stage_end(i, top)
        if i + 1 < len(stages):
            stage_start(i + 1, top)
    step = CFL / jnp.broadcast_to(jnp.max(top, axis=1, keepdims=True), (1, CY))
    step_out[0] = jnp.max(step)
    semi = 0.5 * step

    for k in range(CHUNKS):
        for c in range(3):
            half[5 + c, k] = state[5 + c, k] - semi * change[5 + c, k]
    for k in range(CHUNKS):
        rho, pres = state[0, k], state[4, k]
        vel = [state[1 + c, k] for c in range(3)]
        mag = [cell[c, k] for c in range(3)]
        energy = (
            1.5 * pres
            + (0.5 * rho) * (vel[0] * vel[0] + vel[1] * vel[1] + vel[2] * vel[2])
            + 0.5 * (mag[0] * mag[0] + mag[1] * mag[1] + mag[2] * mag[2])
        )
        if k < EDGE:
            result[0, k] = energy[0:8]
        hrho = rho - semi * change[0, k]
        inv = 1.0 / hrho
        mom = [rho * vel[c] - semi * change[1 + c, k] for c in range(3)]
        energy = energy - semi * change[4, k]
        hmag = [0.5 * (half[5 + c, k] + shifted(half, 5 + c, k, -1, c)) for c in range(3)]
        msq = mom[0] * mom[0] + mom[1] * mom[1] + mom[2] * mom[2]
        bsq = hmag[0] * hmag[0] + hmag[1] * hmag[1] + hmag[2] * hmag[2]
        half[0, k] = hrho
        for c in range(3):
            half[1 + c, k] = mom[c] * inv
            hcell[c, k] = hmag[c]
        half[4, k] = (GAMMA - 1.0) * (energy - 0.5 * (msq * inv) - 0.5 * bsq)

    for c in range(3):
        one, two = (c + 1) % 3, (c + 2) % 3
        names = [(half, 0), (half, 1 + c), (half, 1 + one), (half, 1 + two), (half, 4),
                 (hcell, one), (hcell, two)]
        for k in range(CHUNKS):
            for i, (ref, v) in enumerate(names):
                q = ref[v, k]
                a = q - shifted(ref, v, k, 1, c)
                b = shifted(ref, v, k, -1, c) - q
                g = 0.5 * (
                    jnp.maximum(jnp.minimum(a, b), 0.0) + jnp.minimum(jnp.maximum(a, b), 0.0)
                )
                lefts[7 * c + i, k] = q + g
                rights[7 * c + i, k] = q - g
        for k in range(CHUNKS):
            left = [shifted(lefts, 7 * c + i, k, 1, c) for i in range(7)]
            right = [rights[7 * c + i, k] for i in range(7)]
            put_flux(flux, c, k, hlle(left, right, half[5 + c, k]))
    edges(flux, edge, range(CHUNKS))
    for z in range(CZ):
        rho = state[0, z, 0:8]
        for v in range(5):
            start = rho if v == 0 else result[0, z] if v == 4 else rho * state[v, z, 0:8]
            value = start - step * div_part(flux, v, z)[0:8]
            if v == 0:
                rho_out[z] = value
            elif v == 4:
                ener_out[z] = value
            else:
                mom_out[v - 1, z] = value
        for c in range(3):
            face_out[c, z] = state[5 + c, z, 0:8] - step * curl_parts(edge, c, z)[0:8]

    for copy in sends:
        copy.wait_send()
    for copies in started:
        for copy in copies:
            copy.wait_send()


def hand_on(*refs):
    sem = refs[8]
    copies = [pltpu.make_async_copy(refs[i], refs[4 + i], sem.at[i]) for i in range(4)]
    for copy in copies:
        copy.start()
    for copy in copies:
        copy.wait()


def on_device(nbx, nby, density, velocity, pressure, field):
    stages = max_stages(nbx, nby)
    slots = sum(len(s) for s in stages)
    sides = 1 if nby == 2 else 2
    f32 = jnp.float32
    wide = (CHUNKS, 2 * CX, CY)
    out = pl.pallas_call(
        functools.partial(kernel, nbx, nby, stages),
        out_shape=[
            jax.ShapeDtypeStruct((CZ, CX, CY), f32),
            jax.ShapeDtypeStruct((3, CZ, CX, CY), f32),
            jax.ShapeDtypeStruct((CZ, CX, CY), f32),
            jax.ShapeDtypeStruct((3, CZ, CX, CY), f32),
            jax.ShapeDtypeStruct((1,), f32),
        ],
        in_specs=[pl.BlockSpec(memory_space=pl.ANY)] * 4,
        out_specs=[pl.BlockSpec(memory_space=pltpu.VMEM)] * 4
        + [pl.BlockSpec(memory_space=pltpu.SMEM)],
        scratch_shapes=[
            pltpu.VMEM((8, CZ, CX, CY), f32),
            pltpu.VMEM((8, CX, CY), f32),
            pltpu.VMEM((CZ, CX, CY), f32),
            pltpu.VMEM((CX, CY), f32),
            pltpu.VMEM((8, CZ, CX, CY), f32),
            pltpu.VMEM((sides, 8, CX, CY), f32),
            pltpu.VMEM((sides, 8, CX, CY), f32),
            pltpu.VMEM((len(stages), 1, CY), f32),
            pltpu.VMEM((slots, 1, CY), f32),
            pltpu.VMEM((8,) + wide, f32),
            pltpu.VMEM((3,) + wide, f32),
            pltpu.VMEM((21,) + wide, f32),
            pltpu.VMEM((3,) + wide, f32),
            pltpu.VMEM((8,) + wide, f32),
            pltpu.VMEM((8,) + wide, f32),
            pltpu.VMEM((3,) + wide, f32),
            pltpu.VMEM((21,) + wide, f32),
            pltpu.VMEM((21,) + wide, f32),
            pltpu.VMEM((1, CZ, CX, CY), f32),
            pltpu.SemaphoreType.DMA((4,)),
            pltpu.SemaphoreType.DMA((4,)),
            pltpu.SemaphoreType.DMA((len(HALOS),)),
            pltpu.SemaphoreType.DMA((len(HALOS),)),
            pltpu.SemaphoreType.DMA((slots,)),
            pltpu.SemaphoreType.DMA((slots,)),
        ],
        compiler_params=pltpu.CompilerParams(
            collective_id=0, has_side_effects=True, vmem_limit_bytes=60 * 1024 * 1024
        ),
    )(density, velocity, pressure, field)
    final = pl.pallas_call(
        hand_on,
        out_shape=[jax.ShapeDtypeStruct(a.shape, f32) for a in out[:4]],
        in_specs=[pl.BlockSpec(memory_space=pltpu.VMEM)] * 4,
        out_specs=[pl.BlockSpec(memory_space=pl.ANY)] * 4,
        scratch_shapes=[pltpu.SemaphoreType.DMA((4,))],
    )(*out[:4])
    return (*final, out[4].reshape(()))


def solution(mesh):
    in_specs = (
        P(None, "bx", "by"),
        P(None, None, "bx", "by"),
        P(None, "bx", "by"),
        P(None, None, "bx", "by"),
    )
    out_specs = in_specs + (P(),)
    return jax.shard_map(
        functools.partial(on_device, mesh.shape["bx"], mesh.shape["by"]),
        mesh=mesh, in_specs=in_specs, out_specs=out_specs, check_vma=False,
    )
```

```python
import functools

import jax
import jax.numpy as jnp
from jax import lax
from jax.experimental import pallas as pl
from jax.experimental.pallas import tpu as pltpu
from jax.sharding import PartitionSpec as P

GAMMA = 5.0 / 3.0
CFL = 0.3
TINY = 1e-30
CZ, CX, CY = 4, 8, 128
EDGE = 4
CHUNKS = 5
HALOS = ((-1, 0), (0, -1), (1, 0), (-1, 0), (1, 1), (-1, 1), (0, 1), (1, -1), (-1, -1), (0, -1))


def max_stages(nbx, nby):
    if nbx * nby <= 32:
        return [[(0, y) for y in range(1, nby)], [(x, 0) for x in range(1, nbx)]]
    stages = [[(0, o) for o in range(1, nby)]]
    window = 1
    while window < nbx:
        stages.append([(m * window, 0) for m in (1, 2, 3) if m * window < nbx])
        window *= 4
    return [s for s in stages if s]


def roll(a, by, axis):
    by = by % a.shape[axis]
    return a if by == 0 else pltpu.roll(a, by, axis)


def lanes():
    return lax.broadcasted_iota(jnp.int32, (1, CY), 1)


def shifted(ref, v, k, by, c):
    if c == 0:
        return roll(ref[v, k], by, 0)
    if c == 2:
        return ref[v, (k - by) % CZ] if k < EDGE else roll(ref[v, k], 32 * by, 1)
    body = roll(ref[v, k], by, 1)
    if k == EDGE:
        return body
    if by == 1:
        return jnp.where(lanes() == 0, roll(ref[v, EDGE], -(32 * k + 7), 1), body)
    return jnp.where(lanes() == CY - 1, roll(ref[v, EDGE], CY - 1 - (32 * k + 24), 1), body)


def root(y):
    return y * lax.rsqrt(jnp.maximum(y, TINY))


def fast(rho, pres, n, t):
    a = GAMMA * pres
    s = a + n
    d = a - n
    x = 0.5 * (s + t + root(d * d + t * (t + 2.0 * s)))
    return x * lax.rsqrt(jnp.maximum(x * rho, TINY))


def part(side, bn, n, fastness, alpha_term, w):
    rho, vn, v1, v2, p, b1, b2, t = side
    half_bsq = 0.5 * (t + n)
    energy = 1.5 * p + (0.5 * rho) * (vn * vn + v1 * v1 + v2 * v2) + half_bsq
    wp = w * (p + half_bsq)
    beta = w * bn
    alpha = w * vn + alpha_term
    m = alpha * rho
    vb = vn * bn + v1 * b1 + v2 * b2
    return [
        m,
        m * vn - beta * bn + wp,
        m * v1 - beta * b1,
        m * v2 - beta * b2,
        alpha * energy + wp * vn - beta * vb,
        alpha * b1 - beta * v1,
        alpha * b2 - beta * v2,
    ]


def hlle(left, right, bn):
    n = bn * bn
    left = left + [left[5] * left[5] + left[6] * left[6]]
    right = right + [right[5] * right[5] + right[6] * right[6]]
    cl = fast(left[0], left[4], n, left[7])
    cr = fast(right[0], right[4], n, right[7])
    sl = jnp.minimum(jnp.minimum(left[1] - cl, right[1] - cr), 0.0)
    sr = jnp.maximum(jnp.maximum(left[1] + cl, right[1] + cr), 0.0)
    inv = 1.0 / (sr - sl)
    wl = sr * inv
    wr = -sl * inv
    wd = sl * wl
    fl = part(left, bn, n, cl, -wd, wl)
    fr = part(right, bn, n, cr, wd, wr)
    return [a + b for a, b in zip(fl, fr)]


def put_flux(flux, c, k, values):
    one, two = (c + 1) % 3, (c + 2) % 3
    for slot, value in zip((0, 1 + c, 1 + one, 1 + two, 4, 5, 6), values):
        flux[7 * c + slot, k] = value


def curl_parts(edge, c, k):
    one, two = (c + 1) % 3, (c + 2) % 3
    return (shifted(edge, two, k, -1, one) - edge[two, k]) - (
        shifted(edge, one, k, -1, two) - edge[one, k]
    )


def edges(flux, edge, ks):
    for k in ks:
        for e in range(3):
            a, b = (e + 1) % 3, (e + 2) % 3
            fa, fb = 7 * a + 5, 7 * b + 6
            edge[e, k] = 0.25 * (
                (flux[fb, k] + shifted(flux, fb, k, 1, a))
                - (flux[fa, k] + shifted(flux, fa, k, 1, b))
            )


def div_part(flux, v, k):
    total = None
    for c in range(3):
        term = shifted(flux, 7 * c + v, k, -1, c) - flux[7 * c + v, k]
        total = term if total is None else total + term
    return total


def strips(tiles):
    lane = lanes()
    merged = roll(tiles[0], 8, 1)
    for z in range(1, CZ):
        merged = jnp.where(lane >= 32 * z, roll(tiles[z], 8 + 32 * z, 1), merged)
    return jnp.where(lane % 32 < 16, merged, roll(merged, 16, 1))


def kernel(
    nbx, nby, stages, early,
    rho_in, vel_in, pres_in, face_in,
    rho_out, mom_out, ener_out, face_out, step_out,
    own, own_strip, x_edge, y_edge, halo, y_strip, d_strip, top_send, top_recv,
    state, cell, flux, edge, change, half, hcell, lefts, rights, result,
    in_sem, out_sem, send_sem, recv_sem, tsend_sem, trecv_sem,
):
    mx, my = lax.axis_index("bx"), lax.axis_index("by")

    def at(dx, dy):
        return (lax.rem(mx + dx % nbx, nbx), lax.rem(my + dy % nby, nby))

    loads = [
        pltpu.make_async_copy(rho_in, own.at[0], in_sem.at[0]),
        pltpu.make_async_copy(vel_in, own.at[pl.ds(1, 3)], in_sem.at[1]),
        pltpu.make_async_copy(pres_in, own.at[4], in_sem.at[2]),
        pltpu.make_async_copy(face_in, own.at[pl.ds(5, 3)], in_sem.at[3]),
    ]
    for copy in loads:
        copy.start()

    barrier = pltpu.get_barrier_semaphore()
    greeted = sorted(
        {(dx % nbx, dy % nby) for dx, dy in HALOS}
        | {((-dx) % nbx, (-dy) % nby) for stage in stages for dx, dy in stage}
    )
    for dx, dy in greeted:
        pl.semaphore_signal(
            barrier, inc=1, device_id=at(dx, dy), device_id_type=pl.DeviceIdType.MESH
        )
    for copy in loads:
        copy.wait()
    for v in range(8):
        own_strip[v] = strips([own[v, z] for z in range(CZ)])
    pl.semaphore_wait(barrier, len(greeted))

    low, high = pl.ds(0, 4), pl.ds(4, 4)
    other = 0 if nby == 2 else 1
    plan = [
        (own.at[5, :, pl.ds(0, 1), :], x_edge.at[:, pl.ds(0, 1), :]),
        (own_strip.at[6], y_edge),
        (own.at[:, :, high, :], halo.at[:, :, high, :]),
        (own.at[:, :, low, :], halo.at[:, :, low, :]),
        (own_strip.at[:, high, :], d_strip.at[0, :, high, :]),
        (own_strip.at[:, low, :], d_strip.at[0, :, low, :]),
        (own_strip, y_strip.at[0]),
        (own_strip.at[:, high, :], d_strip.at[other, :, high, :]),
        (own_strip.at[:, low, :], d_strip.at[other, :, low, :]),
        (own_strip, y_strip.at[other]),
    ]
    if nby == 2:
        plan = plan[:7]
    sends = [
        pltpu.make_async_remote_copy(
            src_ref=src, dst_ref=dst, send_sem=send_sem.at[i], recv_sem=recv_sem.at[i],
            device_id=at(*HALOS[i]), device_id_type=pl.DeviceIdType.MESH,
        )
        for i, (src, dst) in enumerate(plan)
    ]
    for copy in sends:
        copy.start()
    for copy in sends[:2]:
        copy.wait_recv()

    best = None
    last_row = lax.broadcasted_iota(jnp.int32, (CX, 1), 0) == CX - 1
    last_lane = lanes() == CY - 1
    for z in range(CZ):
        rho, pres = own[0, z], own[4, z]
        face = [own[5 + c, z] for c in range(3)]
        after = [
            jnp.where(last_row, x_edge[z, 0:1], roll(face[0], -1, 0)),
            jnp.where(last_lane, roll(y_edge[...], CY - 1 - (32 * z + 24), 1), roll(face[1], -1, 1)),
            own[7, (z + 1) % CZ],
        ]
        mag = [0.5 * (face[c] + after[c]) for c in range(3)]
        sq = [m * m for m in mag]
        for c in range(3):
            value = jnp.abs(own[1 + c, z]) + fast(rho, pres, sq[c], sq[(c + 1) % 3] + sq[(c + 2) % 3])
            best = value if best is None else jnp.maximum(best, value)
    top = jnp.max(best, axis=0, keepdims=True)

    first_slot = [sum(len(s) for s in stages[:i]) for i in range(len(stages))]
    started = []

    def stage_start(i, value):
        top_send[i] = value
        copies = []
        for j, (dx, dy) in enumerate(stages[i]):
            slot = first_slot[i] + j
            copy = pltpu.make_async_remote_copy(
                src_ref=top_send.at[i], dst_ref=top_recv.at[slot],
                send_sem=tsend_sem.at[slot], recv_sem=trecv_sem.at[slot],
                device_id=at(dx, dy), device_id_type=pl.DeviceIdType.MESH,
            )
            copy.start()
            copies.append(copy)
        started.append(copies)

    def stage_end(i, value):
        for copy in started[i]:
            copy.wait_recv()
        for j in range(len(stages[i])):
            value = jnp.maximum(value, top_recv[first_slot[i] + j])
        return value

    stage_start(0, top)
    for i in range(early):
        top = stage_end(i, top)
        stage_start(i + 1, top)
    for copy in sends[2:]:
        copy.wait_recv()

    lane = lanes() % 32
    for v in range(8):
        for z in range(CZ):
            state[v, z, 0:8] = own[v, z]
            state[v, z, 8:16] = halo[v, z]
        state[v, EDGE, 0:8] = jnp.where(
            lane < 8, y_strip[0, v], jnp.where(lane < 24, own_strip[v], y_strip[other, v])
        )
        state[v, EDGE, 8:16] = jnp.where(
            lane < 8,
            d_strip[0, v],
            jnp.where(lane < 24, strips([halo[v, z] for z in range(CZ)]), d_strip[other, v]),
        )
    for k in range(CHUNKS):
        for c in range(3):
            cell[c, k] = 0.5 * (state[5 + c, k] + shifted(state, 5 + c, k, -1, c))

    for c in range(3):
        one, two = (c + 1) % 3, (c + 2) % 3
        for k in range(CHUNKS):
            names = [(state, 0), (state, 1 + c), (state, 1 + one), (state, 1 + two), (state, 4),
                     (cell, one), (cell, two)]
            left = [shifted(ref, v, k, 1, c) for ref, v in names]
            right = [ref[v, k] for ref, v in names]
            put_flux(flux, c, k, hlle(left, right, state[5 + c, k]))
    edges(flux, edge, range(CHUNKS))
    for k in range(CHUNKS):
        for v in range(5):
            change[v, k] = div_part(flux, v, k)
        for c in range(3):
            change[5 + c, k] = curl_parts(edge, c, k)
    for i in range(early, len(stages)):
        top = stage_end(i, top)
        if i + 1 < len(stages):
            stage_start(i + 1, top)
    step = CFL / jnp.broadcast_to(jnp.max(top, axis=1, keepdims=True), (1, CY))
    step_out[0] = jnp.max(step)
    semi = 0.5 * step

    for k in range(CHUNKS):
        for c in range(3):
            half[5 + c, k] = state[5 + c, k] - semi * change[5 + c, k]
    for k in range(CHUNKS):
        rho, pres = state[0, k], state[4, k]
        vel = [state[1 + c, k] for c in range(3)]
        mag = [cell[c, k] for c in range(3)]
        energy = (
            1.5 * pres
            + (0.5 * rho) * (vel[0] * vel[0] + vel[1] * vel[1] + vel[2] * vel[2])
            + 0.5 * (mag[0] * mag[0] + mag[1] * mag[1] + mag[2] * mag[2])
        )
        if k < EDGE:
            result[0, k] = energy[0:8]
        hrho = rho - semi * change[0, k]
        inv = 1.0 / hrho
        mom = [rho * vel[c] - semi * change[1 + c, k] for c in range(3)]
        energy = energy - semi * change[4, k]
        hmag = [0.5 * (half[5 + c, k] + shifted(half, 5 + c, k, -1, c)) for c in range(3)]
        msq = mom[0] * mom[0] + mom[1] * mom[1] + mom[2] * mom[2]
        bsq = hmag[0] * hmag[0] + hmag[1] * hmag[1] + hmag[2] * hmag[2]
        half[0, k] = hrho
        for c in range(3):
            half[1 + c, k] = mom[c] * inv
            hcell[c, k] = hmag[c]
        half[4, k] = (GAMMA - 1.0) * (energy - 0.5 * (msq * inv) - 0.5 * bsq)

    for c in range(3):
        one, two = (c + 1) % 3, (c + 2) % 3
        names = [(half, 0), (half, 1 + c), (half, 1 + one), (half, 1 + two), (half, 4),
                 (hcell, one), (hcell, two)]
        for k in range(CHUNKS):
            for i, (ref, v) in enumerate(names):
                q = ref[v, k]
                a = q - shifted(ref, v, k, 1, c)
                b = shifted(ref, v, k, -1, c) - q
                g = 0.5 * (
                    jnp.maximum(jnp.minimum(a, b), 0.0) + jnp.minimum(jnp.maximum(a, b), 0.0)
                )
                lefts[7 * c + i, k] = q + g
                rights[7 * c + i, k] = q - g
        for k in range(CHUNKS):
            left = [shifted(lefts, 7 * c + i, k, 1, c) for i in range(7)]
            right = [rights[7 * c + i, k] for i in range(7)]
            put_flux(flux, c, k, hlle(left, right, half[5 + c, k]))
    edges(flux, edge, range(CHUNKS))
    for z in range(CZ):
        rho = state[0, z, 0:8]
        for v in range(5):
            start = rho if v == 0 else result[0, z] if v == 4 else rho * state[v, z, 0:8]
            value = start - step * div_part(flux, v, z)[0:8]
            if v == 0:
                rho_out[z] = value
            elif v == 4:
                ener_out[z] = value
            else:
                mom_out[v - 1, z] = value
        for c in range(3):
            face_out[c, z] = state[5 + c, z, 0:8] - step * curl_parts(edge, c, z)[0:8]

    for copy in sends:
        copy.wait_send()
    for copies in started:
        for copy in copies:
            copy.wait_send()


def hand_on(*refs):
    sem = refs[8]
    copies = [pltpu.make_async_copy(refs[i], refs[4 + i], sem.at[i]) for i in range(4)]
    for copy in copies:
        copy.start()
    for copy in copies:
        copy.wait()


def on_device(nbx, nby, density, velocity, pressure, field):
    stages = max_stages(nbx, nby)
    slots = sum(len(s) for s in stages)
    sides = 1 if nby == 2 else 2
    f32 = jnp.float32
    wide = (CHUNKS, 2 * CX, CY)
    out = pl.pallas_call(
        functools.partial(kernel, nbx, nby, stages, len(stages) - 1),
        out_shape=[
            jax.ShapeDtypeStruct((CZ, CX, CY), f32),
            jax.ShapeDtypeStruct((3, CZ, CX, CY), f32),
            jax.ShapeDtypeStruct((CZ, CX, CY), f32),
            jax.ShapeDtypeStruct((3, CZ, CX, CY), f32),
            jax.ShapeDtypeStruct((1,), f32),
        ],
        in_specs=[pl.BlockSpec(memory_space=pl.ANY)] * 4,
        out_specs=[pl.BlockSpec(memory_space=pltpu.VMEM)] * 4
        + [pl.BlockSpec(memory_space=pltpu.SMEM)],
        scratch_shapes=[
            pltpu.VMEM((8, CZ, CX, CY), f32),
            pltpu.VMEM((8, CX, CY), f32),
            pltpu.VMEM((CZ, CX, CY), f32),
            pltpu.VMEM((CX, CY), f32),
            pltpu.VMEM((8, CZ, CX, CY), f32),
            pltpu.VMEM((sides, 8, CX, CY), f32),
            pltpu.VMEM((sides, 8, CX, CY), f32),
            pltpu.VMEM((len(stages), 1, CY), f32),
            pltpu.VMEM((slots, 1, CY), f32),
            pltpu.VMEM((8,) + wide, f32),
            pltpu.VMEM((3,) + wide, f32),
            pltpu.VMEM((21,) + wide, f32),
            pltpu.VMEM((3,) + wide, f32),
            pltpu.VMEM((8,) + wide, f32),
            pltpu.VMEM((8,) + wide, f32),
            pltpu.VMEM((3,) + wide, f32),
            pltpu.VMEM((21,) + wide, f32),
            pltpu.VMEM((21,) + wide, f32),
            pltpu.VMEM((1, CZ, CX, CY), f32),
            pltpu.SemaphoreType.DMA((4,)),
            pltpu.SemaphoreType.DMA((4,)),
            pltpu.SemaphoreType.DMA((len(HALOS),)),
            pltpu.SemaphoreType.DMA((len(HALOS),)),
            pltpu.SemaphoreType.DMA((slots,)),
            pltpu.SemaphoreType.DMA((slots,)),
        ],
        compiler_params=pltpu.CompilerParams(
            collective_id=0, has_side_effects=True, vmem_limit_bytes=60 * 1024 * 1024
        ),
    )(density, velocity, pressure, field)
    final = pl.pallas_call(
        hand_on,
        out_shape=[jax.ShapeDtypeStruct(a.shape, f32) for a in out[:4]],
        in_specs=[pl.BlockSpec(memory_space=pltpu.VMEM)] * 4,
        out_specs=[pl.BlockSpec(memory_space=pl.ANY)] * 4,
        scratch_shapes=[pltpu.SemaphoreType.DMA((4,))],
    )(*out[:4])
    return (*final, out[4].reshape(()))


def solution(mesh):
    in_specs = (
        P(None, "bx", "by"),
        P(None, None, "bx", "by"),
        P(None, "bx", "by"),
        P(None, None, "bx", "by"),
    )
    out_specs = in_specs + (P(),)
    return jax.shard_map(
        functools.partial(on_device, mesh.shape["bx"], mesh.shape["by"]),
        mesh=mesh, in_specs=in_specs, out_specs=out_specs, check_vma=False,
    )
```
